256 devices in a mesh: member: 16 (over z, core), region: 16 (over y, x).
Axes of the slice: x: 4, y: 4, z: 8, core: 2. Of those that a mesh axis runs over, the one named last changes fastest.
Arguments:
- prior_states: bfloat16 [512, 524288], P('member', 'region'), may hold values from -6 to 6
- measured_values: bfloat16 [65536], P('region'), may hold values from -12 to 12
- measurement_precision: bfloat16 [65536], P('region'), may hold values from 0.5 to 4
- measured_subgrid_line: int32 [65536], P('region'), may hold values from 0 to 32767, as said below
- neighbour_measurement_lookup: int32 [16, 16, 1024], P('region'), may hold values from 0 to 12287, as said below
- active_entries_tally: int32 [16, 16], P('region', 'member'), may hold values from 512 to 1024, as said below
- distance_tier: int32 [16, 16, 1024], P('region', 'member'), may hold values from 0 to 8
- eastward_weight_share: int32 [16, 16, 2048], P('region', 'member'), may hold values from 0 to 8
Outputs:
- analysis: bfloat16 [512, 524288], P('member', 'region')
The draws below stay inside these ranges and needn't reach their ends.
Inputs may be any that keep to these rules, and one draw needn't show every extreme that they name: `neighbour_measurement_lookup`: for coarse point (s, p) the live and dead slots name distinct observations, all in blocks p-1, p, p+1 (each block 256 observations of a sector, in order) of sectors s-1, s, s+1; blocks outside 0 to 15 are never named. `measured_subgrid_line`: observation o of a sector measures a row of its block: from ((o % 4096) // 256) * 2048 to that plus 2048 - 1. `active_entries_tally`: some coarse point has all 1024 slots live.
All inputs are finite; a program needn't handle non-finite values.
Results may differ from the reference program's by a relative error of at most 0.019.
Values may be sent and summed in bfloat16 or wider, within the bound.
A program may use at most 64 MiB of HBM per device.

```python
import math
import jax
import jax.numpy as jnp
from jax import lax

ENSEMBLE_SIZE = 512
LOC = 1024
ITERS = 6
OBS_CP = 256
SUBGRID_EACH = 2048
CP_TILE = 16
SECTORS = 16
OBS_ALL = 65536
SUBGRID_ALL = 524288
N_MEMBER = 16
N_REGION = 16


def draw_neighbour_measurement_lookup(key, part):
    latitude_swaths = N_MEMBER
    region_dimension = N_REGION
    obs_tile = OBS_CP * latitude_swaths
    cands = 9 * OBS_CP
    number = jnp.arange(cands, dtype=jnp.int32)
    side = number // (3 * OBS_CP)
    offset = number // OBS_CP % 3
    inside = number % OBS_CP
    coarse = jnp.arange(latitude_swaths, dtype=jnp.int32)[:, None]
    block = coarse + offset[None, :] - 1
    valid = (block >= 0) & (block < latitude_swaths)
    scores = jax.random.randint(key, (region_dimension, latitude_swaths, cands), 0, 65536) * cands + number
    scores = jnp.where(valid[None], scores, scores + 2 ** 30)
    order = jnp.argsort(scores, axis=-1, stable=True)[..., :LOC]
    table = side[None, :] * obs_tile + jnp.clip(block, 0, latitude_swaths - 1) * OBS_CP + inside[None, :]
    table = jnp.broadcast_to(table[None], (region_dimension, latitude_swaths, cands))
    return jnp.take_along_axis(table, order, axis=-1).astype(jnp.int32)


def draw_measured_subgrid_line(key, part):
    total = N_REGION * OBS_CP * N_MEMBER
    number = jnp.arange(total, dtype=jnp.int32)
    block = number % (OBS_CP * N_MEMBER) // OBS_CP
    return (block * SUBGRID_EACH + jax.random.randint(key, (total,), 0, SUBGRID_EACH)).astype(jnp.int32)


def draw_active_entries_tally(key, part):
    total = N_REGION * N_MEMBER
    counts = jax.random.randint(key, (total,), LOC // 2, LOC + 1)
    chosen_spot = jax.random.randint(jax.random.fold_in(key, 7), (), 0, total)
    counts = jnp.where(jnp.arange(total, dtype=jnp.int32) == chosen_spot, LOC, counts)
    return counts.reshape(N_REGION, N_MEMBER).astype(jnp.int32)


def with_ends(entries, key, least, largest):
    shape = entries.shape
    place = [jax.random.randint(jax.random.fold_in(key, axis), (), 0, shape[axis]) for axis in range(len(shape))]
    entries = entries.at[tuple(place)].set(least)
    longest = shape.index(max(shape))
    place[longest] = (place[longest] + 1) % shape[longest]
    return entries.at[tuple(place)].set(largest)


def steps_of(stream_key, shape, shards, low, top_value):
    gain = 1.0
    for axis_at, parts in shards:
        draws = jax.random.uniform(jax.random.fold_in(jax.random.fold_in(stream_key, 6), axis_at), (parts,), jnp.float32, low / len(shards), top_value / len(shards))
        gain = gain * jnp.repeat(jnp.exp(draws), shape[axis_at] // parts).reshape((-1,) + (1,) * (len(shape) - 1 - axis_at))
    return gain


def bell_draw(rng, extent, deviation, reach, split=(), kind=jnp.bfloat16):
    entries = deviation * jax.random.normal(rng, extent, jnp.float32)
    if split:
        entries = entries * steps_of(rng, extent, split, -0.22, 0.18)
    return jnp.clip(entries, -reach, reach).astype(kind)


def setup_inputs(seed: int = 0) -> dict:
    key_of = jax.random.split(jax.random.key(seed), 9)
    return {
        "prior_states": bell_draw(key_of[0], (ENSEMBLE_SIZE, SUBGRID_ALL), 1.0, 6.0, ((0, 16), (1, 16))),
        "measured_values": bell_draw(key_of[1], (OBS_ALL,), 2.0, 12.0, ((0, 16),)),
        "measurement_precision": jnp.clip(jnp.exp(math.log(4.0) - 2.0794415 * jax.random.uniform(key_of[2], (OBS_ALL,), jnp.float32) ** steps_of(key_of[2], (OBS_ALL,), ((0, 16),), -0.2, 0.2)), 0.5, 4.0).astype(jnp.bfloat16),
        "measured_subgrid_line": draw_measured_subgrid_line(jax.random.fold_in(key_of[8], 71), 0),
        "neighbour_measurement_lookup": draw_neighbour_measurement_lookup(jax.random.fold_in(key_of[8], 71), 0),
        "active_entries_tally": draw_active_entries_tally(jax.random.fold_in(key_of[8], 71), 0),
        "distance_tier": with_ends(jax.random.randint(key_of[6], (SECTORS, CP_TILE, LOC), 0, 9), jax.random.fold_in(key_of[6], 1), 0, 8).astype(jnp.int32),
        "eastward_weight_share": with_ends(jax.random.randint(key_of[7], (SECTORS, CP_TILE, SUBGRID_EACH), 0, 9), jax.random.fold_in(key_of[7], 1), 0, 8).astype(jnp.int32),
    }


def transform(chosen, obs_val, obs_w, count, dist):
    ensemble_dimension = chosen.shape[0]
    slots = chosen.shape[1]
    values = chosen.astype(jnp.float32)
    ybar = lax.optimization_barrier(jnp.mean(values, axis=0))
    pert = (values - ybar).astype(jnp.bfloat16)
    live = (jnp.arange(slots, dtype=jnp.int32) < count).astype(jnp.float32)
    wts = obs_w.astype(jnp.float32) * 2.0 / (2.0 + dist.astype(jnp.float32)) * live
    weighted = pert.astype(jnp.float32) * wts
    gram = lax.dot_general(weighted.astype(jnp.bfloat16), pert, (((1,), (1,)), ((), ())), preferred_element_type=jnp.float32)
    identity = jnp.eye(ensemble_dimension, dtype=jnp.float32)
    amat = gram + (ensemble_dimension - 1.0) * identity
    norm = jnp.sqrt(jnp.sum(amat * amat))
    gvec = jnp.dot(weighted, obs_val.astype(jnp.float32) - ybar, precision=lax.Precision.HIGHEST)
    zmat = (amat / norm).astype(jnp.bfloat16)
    ymat = identity.astype(jnp.bfloat16)
    for step in range(ITERS):
        product = jnp.dot(zmat, ymat, preferred_element_type=jnp.float32)
        tmat = (1.5 * identity - 0.5 * product).astype(jnp.bfloat16)
        ynext = jnp.dot(ymat, tmat, preferred_element_type=jnp.float32).astype(jnp.bfloat16)
        zmat = jnp.dot(tmat, zmat, preferred_element_type=jnp.float32).astype(jnp.bfloat16)
        ymat = ynext
    isq = ymat.astype(jnp.float32) / jnp.sqrt(norm)
    wbar = jnp.dot(isq, jnp.dot(isq, gvec, precision=lax.Precision.HIGHEST), precision=lax.Precision.HIGHEST)
    return (jnp.sqrt(ensemble_dimension - 1.0) * isq + wbar[:, None]).astype(jnp.bfloat16)

def update(vertical_dimension, weights, eastern, level):
    values = vertical_dimension.astype(jnp.float32)
    xbar = lax.optimization_barrier(jnp.mean(values, axis=0))
    centred = (values - xbar).astype(jnp.bfloat16)
    dims = (((0,), (0,)), ((), ()))
    own_term = lax.dot_general(weights, centred, dims, preferred_element_type=jnp.float32)
    east_term = lax.dot_general(eastern, centred, dims, preferred_element_type=jnp.float32)
    share = level.astype(jnp.float32) / 8.0
    return (xbar + (1.0 - share) * own_term + share * east_term).astype(jnp.bfloat16)

def reference(prior_states, measured_values, measurement_precision, measured_subgrid_line, neighbour_measurement_lookup, active_entries_tally, distance_tier, eastward_weight_share):
    region_dimension = N_REGION
    latitude_swaths = N_MEMBER
    obs_tile = OBS_CP * latitude_swaths
    fine_tile = SUBGRID_EACH * latitude_swaths
    sector_of = jnp.arange(region_dimension * obs_tile, dtype=jnp.int32) // obs_tile
    lateral_dimension = (sector_of * fine_tile + measured_subgrid_line).astype(jnp.int32)
    mapped_dimension = jnp.take(prior_states, lateral_dimension, axis=1)
    sector_ids = jnp.arange(region_dimension, dtype=jnp.int32)[:, None, None]
    side = neighbour_measurement_lookup // obs_tile
    within = neighbour_measurement_lookup % obs_tile
    global_idx = ((sector_ids + side - 1) % region_dimension * obs_tile + within).astype(jnp.int32)
    flat_idx = global_idx.reshape(region_dimension * latitude_swaths, LOC)

    def coarse(items):
        picks, count, dist = items
        chosen = jnp.take(mapped_dimension, picks, axis=1)
        return transform(chosen, measured_values[picks], measurement_precision[picks], count, dist)
    weights = lax.map(coarse, (flat_idx, active_entries_tally.reshape(region_dimension * latitude_swaths), distance_tier.reshape(region_dimension * latitude_swaths, LOC)))
    eastern = jnp.roll(weights.reshape(region_dimension, latitude_swaths, ENSEMBLE_SIZE, ENSEMBLE_SIZE), -1, axis=0).reshape(region_dimension * latitude_swaths, ENSEMBLE_SIZE, ENSEMBLE_SIZE)
    vertical_dimension = prior_states.reshape(ENSEMBLE_SIZE, region_dimension * latitude_swaths, SUBGRID_EACH).transpose(1, 0, 2)
    levels = eastward_weight_share.reshape(region_dimension * latitude_swaths, SUBGRID_EACH)

    def apply_rows(items):
        return update(items[0], items[1], items[2], items[3])
    result = lax.map(apply_rows, (vertical_dimension, weights, eastern, levels))
    return result.transpose(1, 0, 2).reshape(ENSEMBLE_SIZE, region_dimension * latitude_swaths * SUBGRID_EACH)
```

```python
import functools

import jax
import jax.numpy as jnp
from jax import lax
from jax.experimental import pallas as pl
from jax.experimental.pallas import tpu as pltpu
from jax.sharding import PartitionSpec as P

ITERS = 6
MESH = pl.DeviceIdType.MESH
F32 = jnp.float32
BF16 = jnp.bfloat16
NN = (((1,), (0,)), ((), ()))
NT = (((1,), (1,)), ((), ()))


def dot(a, b, dims=NN):
    return lax.dot_general(a, b, dims, preferred_element_type=F32)


def iota(shape, dim):
    return lax.broadcasted_iota(jnp.int32, shape, dim)


def split_rows(x):
    hi = x.astype(BF16).astype(F32)
    mid = (x - hi).astype(BF16).astype(F32)
    low = x - hi - mid
    row = iota((16, x.shape[1]), 0)
    rows = jnp.where(row == 0, hi, jnp.where(row == 1, mid, jnp.where(row == 2, low, 0.0)))
    return rows.astype(BF16)


def row_dot(x, b, dims):
    return jnp.sum(dot(split_rows(x), b, dims), axis=0, keepdims=True)


def kernel(
    n, regions,
    prior, line, data, lookup, dist, share, count,
    out,
    pv, state, psend, blocks, pert, wp, want, asked, gs, gr, vs, vr, amat, y, z, t, ye, fs, fe, res,
    load_sem, in_s, in_r, pr_s, pr_r, halo_s, halo_r, want_s, want_r, g_s, g_r, v_s, v_r, y_s, y_r, f_s, f_r, out_s, out_r,
):
    p = lax.axis_index("member")
    s = lax.axis_index("region")
    members = 512 // n
    west, east = lax.rem(s + regions - 1, regions), lax.rem(s + 1, regions)

    def remote(src, dst, ss, rs, **where):
        return pltpu.make_async_remote_copy(
            src_ref=src, dst_ref=dst, send_sem=ss, recv_sem=rs, device_id=where, device_id_type=MESH
        )

    def peer(d):
        return lax.rem(p + d, n)

    def my_rows(ref, k):
        return ref.at[pl.ds(pl.multiple_of(k * members, members), members)]

    def band(ref, k):
        return ref.at[:, pl.ds(pl.multiple_of(k * 2048, 2048), 2048)]

    load = pltpu.make_async_copy(prior, pv, load_sem)
    load.start()
    barrier = pltpu.get_barrier_semaphore()

    def greet(d, carry):
        pl.semaphore_signal(barrier, inc=1, device_id={"member": peer(d)}, device_id_type=MESH)
        return carry

    lax.fori_loop(1, n, greet, 0)
    for other in (west, east):
        pl.semaphore_signal(barrier, inc=1, device_id={"region": other}, device_id_type=MESH)

    slots = lookup.shape[-1]
    named = lookup[0, pl.ds(p, 1), :]
    side = lax.shift_right_logical(named, 12)
    offset = (lax.shift_right_logical(named, 8) & 15) - p + 1
    live = iota((1, slots), 1) < count[0, 0]
    code = jnp.where(live, (dist[0] + 1).astype(F32), 0.0)
    group = jnp.where(iota((32, slots), 0) == side * 8 + offset, code, 0.0).astype(BF16)
    place = jnp.where(iota((256, slots), 0) == (named & 255), 1.0, 0.0).astype(BF16)
    want[...] = dot(group, place, NT)

    load.wait()
    pl.semaphore_wait(barrier, n + 1)

    def state_copy(d):
        q = peer(d)
        return remote(band(pv, q), my_rows(state, p), in_s.at[d], in_r.at[d], member=q)

    def send_state(pairs):
        for k in pairs:
            state_copy(k).start()
            if 2 * k != n:
                state_copy(n - k).start()

    send_state((1, 2))
    want_west = remote(want.at[pl.ds(0, 8)], asked.at[1], want_s.at[0], want_r.at[1], region=west)
    want_east = remote(want.at[pl.ds(16, 8)], asked.at[0], want_s.at[1], want_r.at[0], region=east)
    want_west.start()
    want_east.start()

    def project(q):
        rows = [pv[:, pl.ds(pl.multiple_of(q * 2048 + 256 * h, 256), 256)] for h in range(8)]
        at = line[pl.ds(q, 1), :]
        pick = jnp.where(iota((256, 256), 0) == (at & 255), 1.0, 0.0).astype(BF16)
        found = dot(jnp.concatenate(rows, axis=0), pick)
        high = lax.shift_right_logical(at, 8) & 7
        total = jnp.zeros((members, 256), F32)
        for h in range(8):
            total = total + jnp.where(high == h, found[members * h : members * (h + 1)], 0.0)
        return total.astype(BF16)

    def proj_copy(d):
        q = peer(d)
        return remote(psend.at[q], my_rows(blocks.at[1], p), pr_s.at[d], pr_r.at[d], member=q)

    def project_one(d, carry):
        q = peer(d)
        psend[q] = project(q)
        proj_copy(d).start()
        return carry

    lax.fori_loop(1, n, project_one, 0)
    send_state((3, 4))
    blocks[1, pl.ds(pl.multiple_of(p * members, members), members), :] = project(p)
    own = pltpu.make_async_copy(band(pv, p), my_rows(state, p), load_sem)
    own.start()

    def proj_wait(d, carry):
        proj_copy(d).wait_recv()
        return carry

    lax.fori_loop(1, n, proj_wait, 0)
    up = remote(blocks.at[1], blocks.at[0], halo_s.at[0], halo_r.at[0], member=peer(1))
    down = remote(blocks.at[1], blocks.at[2], halo_s.at[1], halo_r.at[1], member=peer(n - 1))
    up.start()
    down.start()
    send_state((5, 6, 7, 8))

    departs, precision = [None] * 3, [None] * 3

    def centre(j):
        values = blocks[j].astype(F32)
        ybar = jnp.mean(values, axis=0, keepdims=True)
        pert[:, 256 * j : 256 * (j + 1)] = (values - ybar).astype(BF16)
        k = lax.rem(p + n - 1 + j, n)
        departs[j] = data[0, pl.ds(k, 1), :] - ybar
        precision[j] = data[1, pl.ds(k, 1), :]

    centre(1)
    up.wait_recv()
    centre(0)
    down.wait_recv()
    centre(2)
    want_west.wait_recv()
    want_east.wait_recv()

    def weigh(asks):
        moments = []
        for j in range(3):
            code = asks[j : j + 1, :]
            w = jnp.where(code > 0.0, precision[j] * 2.0 / (1.0 + code), 0.0)
            cols = slice(256 * j, 256 * (j + 1))
            wp[:, cols] = (pert[:, cols].astype(F32) * w).astype(BF16)
            moments.append(w * departs[j])
        return row_dot(jnp.concatenate(moments, axis=1), pert[...], NT)

    def gram(i):
        return dot(wp[128 * i : 128 * (i + 1), :], pert[128 * i :, :], NT)

    def gram_copy(side, i, where):
        part = (pl.ds(128 * i, 128), pl.ds(128 * i, 512 - 128 * i))
        return remote(gs.at[side].at[part], gr.at[1 - side].at[part], g_s.at[side, i], g_r.at[1 - side, i], region=where)

    def moment_copy(side, where):
        return remote(vs.at[side], vr.at[1 - side], v_s.at[side], v_r.at[1 - side], region=where)

    for side_, where in ((0, west), (1, east)):
        moment = weigh(asked[side_])
        vs[side_] = jnp.broadcast_to(moment, (8, 512))
        moment_copy(side_, where).start()
        for i in range(4):
            gs[side_, 128 * i : 128 * (i + 1), 128 * i :] = gram(i).astype(BF16)
            gram_copy(side_, i, where).start()
    gvec = weigh(want[8:16, :])
    for i in range(4):
        amat[128 * i : 128 * (i + 1), 128 * i :] = gram(i)

    def eye(rows, cols, at):
        return iota((rows, cols), 0) + at == iota((rows, cols), 1)

    squares = jnp.zeros((1, 1), F32)
    for i in range(4):
        for side_, where in ((0, west), (1, east)):
            gram_copy(side_, i, where).wait_recv()
        rows, width = slice(128 * i, 128 * (i + 1)), 512 - 128 * i
        a = amat[rows, 128 * i :] + (gr[0, rows, 128 * i :].astype(F32) + gr[1, rows, 128 * i :].astype(F32))
        a = a + jnp.where(eye(128, width, 0), 511.0, 0.0)
        amat[rows, 128 * i :] = a
        twice = a * a * jnp.where(iota((1, width), 1) < 128, 1.0, 2.0)
        squares = squares + jnp.sum(jnp.sum(twice, axis=0, keepdims=True), axis=1, keepdims=True)
    norm = jnp.sqrt(squares)
    inverse = 1.0 / norm
    for i in range(4):
        rows = slice(128 * i, 128 * (i + 1))
        scaled = amat[rows, 128 * i :] * inverse
        z[0, rows, 128 * i :] = scaled.astype(BF16)
        for j in range(i + 1, 4):
            z[0, 128 * j : 128 * (j + 1), rows] = scaled[:, 128 * (j - i) : 128 * (j - i + 1)].T.astype(BF16)

    half = 256
    halves = [slice(0, half), slice(half, 512)]
    for k, rows in enumerate(halves):
        first = jnp.where(eye(half, 512, half * k), 1.5, 0.0) - 0.5 * z[0, rows, :].astype(F32)
        y[1, rows, :] = first.astype(BF16)
    for rows in halves:
        z[1, rows, :] = dot(y[1, rows, :], z[0]).astype(BF16)

    def make_t(now):
        for k, rows in enumerate(halves):
            product = dot(z[now, rows, :], y[now])
            t[rows, :] = (jnp.where(eye(half, 512, half * k), 1.5, 0.0) - 0.5 * product).astype(BF16)

    def step(it, carry):
        now = lax.rem(it, 2)
        make_t(now)
        for rows in halves:
            y[1 - now, rows, :] = dot(y[now, rows, :], t[...]).astype(BF16)
            z[1 - now, rows, :] = dot(t[rows, :], z[now]).astype(BF16)
        return carry

    lax.fori_loop(1, ITERS - 1, step, 0)
    last = (ITERS - 1) % 2
    make_t(last)
    yf = y.at[1 - last]
    for rows in halves:
        yf[rows, :] = dot(y[last, rows, :], t[...]).astype(BF16)

    def east_copy(d):
        q = peer(d)
        return remote(my_rows(yf, q), my_rows(ye, q), y_s.at[d], y_r.at[d], region=west)

    def east_send(d, carry):
        east_copy(d).start()
        return carry

    lax.fori_loop(0, n, east_send, 0)
    for side_, where in ((0, west), (1, east)):
        moment_copy(side_, where).wait_recv()
    gvec = gvec + (vr[0, 0:1, :] + vr[1, 0:1, :])
    root = jnp.sqrt(norm)
    wbar = row_dot(row_dot(gvec, yf[...], NT) / root, yf[...], NT) / root
    scale = jnp.sqrt(F32(511.0)) / root
    fs[...] = jnp.where(iota((8, 512), 0) == 0, wbar, jnp.broadcast_to(scale, (8, 512)))
    factors = remote(fs, fe, f_s, f_r, region=west)
    factors.start()

    own.wait()

    def state_wait(d, carry):
        state_copy(d).wait_recv()
        return carry

    lax.fori_loop(1, n, state_wait, 0)
    xbars, bases, owns, easts = [], [], [], []
    tile = 512
    for c in range(4):
        cols = slice(tile * c, tile * (c + 1))
        values = state[:, cols].astype(F32)
        xbar = jnp.mean(values, axis=0, keepdims=True)
        state[:, cols] = (values - xbar).astype(BF16)
        xbars.append(xbar)
    factors.wait_recv()
    for c in range(4):
        cols = slice(tile * c, tile * (c + 1))
        part = share[0, :, cols].astype(F32) * 0.125
        shift_own = row_dot(wbar, state[:, cols], NN)
        shift_east = row_dot(fe[0:1, :], state[:, cols], NN)
        bases.append(xbars[c] + (1.0 - part) * shift_own + part * shift_east)
        owns.append((1.0 - part) * scale)
        easts.append(part * fe[1:2, 0:tile])

    def out_copy(d):
        q = peer(d)
        return remote(res.at[q], band(out, p), out_s.at[d], out_r.at[d], member=q)

    def update(q):
        at = pl.ds(pl.multiple_of(q * members, members), members)
        lhs = jnp.concatenate([yf[at, :], ye[at, :]], axis=0)
        for c in range(4):
            cols = slice(tile * c, tile * (c + 1))
            both = dot(lhs, state[:, cols])
            value = bases[c] + owns[c] * both[:members] + easts[c] * both[members:]
            res[q, :, cols] = value.astype(BF16)

    def update_one(d, carry):
        east_copy(d).wait_recv()
        update(peer(d))
        out_copy(d).start()
        return carry

    lax.fori_loop(1, n, update_one, 0)
    east_copy(0).wait_recv()
    update(p)
    mine = pltpu.make_async_copy(res.at[p], band(out, p), load_sem)
    mine.start()

    def finish(d, carry):
        out_copy(d).wait()
        state_copy(d).wait_send()
        proj_copy(d).wait_send()
        east_copy(d).wait_send()
        return carry

    lax.fori_loop(1, n, finish, 0)
    east_copy(0).wait_send()
    mine.wait()
    for c in (want_west, want_east, up, down, factors):
        c.wait_send()
    for side_, where in ((0, west), (1, east)):
        moment_copy(side_, where).wait_send()
        for i in range(4):
            gram_copy(side_, i, where).wait_send()


def local(n, regions, prior, values, precision, line, lookup, count, dist, share):
    data = jnp.stack((values, precision)).astype(F32).reshape(2, n, -1)
    dma = pltpu.SemaphoreType.DMA
    vmem = pl.BlockSpec(memory_space=pltpu.VMEM)
    members = prior.shape[0]
    return pl.pallas_call(
        functools.partial(kernel, n, regions),
        out_shape=jax.ShapeDtypeStruct(prior.shape, BF16),
        in_specs=[pl.BlockSpec(memory_space=pl.ANY)] + [vmem] * 5 + [pl.BlockSpec(memory_space=pltpu.SMEM)],
        out_specs=pl.BlockSpec(memory_space=pl.ANY),
        scratch_shapes=[
            pltpu.VMEM(prior.shape, BF16),
            pltpu.VMEM((512, 2048), BF16),
            pltpu.VMEM((n, members, 256), BF16),
            pltpu.VMEM((3, 512, 256), BF16),
            pltpu.VMEM((512, 768), BF16),
            pltpu.VMEM((512, 768), BF16),
            pltpu.VMEM((32, 256), F32),
            pltpu.VMEM((2, 8, 256), F32),
            pltpu.VMEM((2, 512, 512), BF16),
            pltpu.VMEM((2, 512, 512), BF16),
            pltpu.VMEM((2, 8, 512), F32),
            pltpu.VMEM((2, 8, 512), F32),
            pltpu.VMEM((512, 512), F32),
            pltpu.VMEM((2, 512, 512), BF16),
            pltpu.VMEM((2, 512, 512), BF16),
            pltpu.VMEM((512, 512), BF16),
            pltpu.VMEM((512, 512), BF16),
            pltpu.VMEM((8, 512), F32),
            pltpu.VMEM((8, 512), F32),
            pltpu.VMEM((n, members, 2048), BF16),
            dma,
            dma((n,)), dma((n,)),
            dma((n,)), dma((n,)),
            dma((2,)), dma((2,)),
            dma((2,)), dma((2,)),
            dma((2, 4)), dma((2, 4)),
            dma((2,)), dma((2,)),
            dma((n,)), dma((n,)),
            dma, dma,
            dma((n,)), dma((n,)),
        ],
        compiler_params=pltpu.CompilerParams(
            collective_id=0, has_side_effects=True, vmem_limit_bytes=40 * 1024 * 1024
        ),
    )(prior, line.reshape(n, -1), data, lookup, dist, share, count)


def solution(mesh):
    in_specs = (
        P("member", "region"),
        P("region"),
        P("region"),
        P("region"),
        P("region", None, None),
        P("region", "member"),
        P("region", "member", None),
        P("region", "member", None),
    )
    body = functools.partial(local, mesh.shape["member"], mesh.shape["region"])
    return jax.shard_map(body, mesh=mesh, in_specs=in_specs, out_specs=P("member", "region"), check_vma=False)
```

```python
import functools

import jax
import jax.numpy as jnp
from jax import lax
from jax.experimental import pallas as pl
from jax.experimental.pallas import tpu as pltpu
from jax.sharding import PartitionSpec as P

ITERS = 6
MESH = pl.DeviceIdType.MESH
F32 = jnp.float32
BF16 = jnp.bfloat16
NN = (((1,), (0,)), ((), ()))
NT = (((1,), (1,)), ((), ()))


def dot(a, b, dims=NN):
    return lax.dot_general(a, b, dims, preferred_element_type=F32)


def iota(shape, dim):
    return lax.broadcasted_iota(jnp.int32, shape, dim)


def split_rows(x):
    hi = x.astype(BF16).astype(F32)
    mid = (x - hi).astype(BF16).astype(F32)
    low = x - hi - mid
    row = iota((16, x.shape[1]), 0)
    rows = jnp.where(row == 0, hi, jnp.where(row == 1, mid, jnp.where(row == 2, low, 0.0)))
    return rows.astype(BF16)


def row_dot(x, b, dims):
    return jnp.sum(dot(split_rows(x), b, dims), axis=0, keepdims=True)


def kernel(
    n, regions,
    prior, line_in, values_in, precision_in, lookup_in, dist_in, share_in, count,
    out,
    line, values, precisions, data, lookup, dist, share, pv, state, psend, blocks, pert, wp, want, asked, gs, gr, vs, vr, amat, y, z, t, ye, fs, fe, res,
    load_sem, small_sem, in_s, in_r, pr_s, pr_r, halo_s, halo_r, want_s, want_r, g_s, g_r, v_s, v_r, y_s, y_r, f_s, f_r, out_s, out_r,
):
    p = lax.axis_index("member")
    s = lax.axis_index("region")
    members = 512 // n
    west, east = lax.rem(s + regions - 1, regions), lax.rem(s + 1, regions)

    def remote(src, dst, ss, rs, **where):
        return pltpu.make_async_remote_copy(
            src_ref=src, dst_ref=dst, send_sem=ss, recv_sem=rs, device_id=where, device_id_type=MESH
        )

    def peer(d):
        return lax.rem(p + d, n)

    def my_rows(ref, k):
        return ref.at[pl.ds(pl.multiple_of(k * members, members), members)]

    def band(ref, k):
        return ref.at[:, pl.ds(pl.multiple_of(k * 2048, 2048), 2048)]

    load = pltpu.make_async_copy(prior, pv, load_sem)
    load.start()
    smalls = [
        pltpu.make_async_copy(src, dst, small_sem.at[k])
        for k, (src, dst) in enumerate(
            (
                (lookup_in, lookup),
                (dist_in, dist),
                (line_in, line),
                (values_in, values),
                (precision_in, precisions),
                (share_in, share),
            )
        )
    ]
    for c in smalls:
        c.start()
    barrier = pltpu.get_barrier_semaphore()

    def greet(d, carry):
        pl.semaphore_signal(barrier, inc=1, device_id={"member": peer(d)}, device_id_type=MESH)
        return carry

    lax.fori_loop(1, n, greet, 0)
    for other in (west, east):
        pl.semaphore_signal(barrier, inc=1, device_id={"region": other}, device_id_type=MESH)

    def pair(ref, k):
        return jnp.concatenate([ref[pl.ds(2 * k, 1), :], ref[pl.ds(2 * k + 1, 1), :]], axis=1)

    for c in smalls:
        c.wait()
    data[0:32, :] = values[...].astype(F32)
    data[32:64, :] = precisions[...].astype(F32)

    slots = lookup.shape[-1]
    named = lookup[0, pl.ds(p, 1), :]
    side = lax.shift_right_logical(named, 12)
    offset = (lax.shift_right_logical(named, 8) & 15) - p + 1
    live = iota((1, slots), 1) < count[0, 0]
    code = jnp.where(live, (dist[0] + 1).astype(F32), 0.0)
    group = jnp.where(iota((32, slots), 0) == side * 8 + offset, code, 0.0).astype(BF16)
    place = jnp.where(iota((256, slots), 0) == (named & 255), 1.0, 0.0).astype(BF16)
    want[...] = dot(group, place, NT)

    def project(q):
        rows = [pv[:, pl.ds(pl.multiple_of(q * 2048 + 256 * h, 256), 256)] for h in range(8)]
        at = pair(line, q)
        pick = jnp.where(iota((256, 256), 0) == (at & 255), 1.0, 0.0).astype(BF16)
        found = dot(jnp.concatenate(rows, axis=0), pick)
        high = lax.shift_right_logical(at, 8) & 7
        total = jnp.zeros((members, 256), F32)
        for h in range(8):
            total = total + jnp.where(high == h, found[members * h : members * (h + 1)], 0.0)
        return total.astype(BF16)

    load.wait()

    def project_one(q, carry):
        psend[q] = project(q)
        return carry

    lax.fori_loop(0, n, project_one, 0)
    pl.semaphore_wait(barrier, n + 1)

    def state_copy(d):
        q = peer(d)
        return remote(band(pv, q), my_rows(state, p), in_s.at[d], in_r.at[d], member=q)

    def send_state(pairs):
        for k in pairs:
            state_copy(k).start()
            if 2 * k != n:
                state_copy(n - k).start()

    want_west = remote(want.at[pl.ds(0, 8)], asked.at[1], want_s.at[0], want_r.at[1], region=west)
    want_east = remote(want.at[pl.ds(16, 8)], asked.at[0], want_s.at[1], want_r.at[0], region=east)

    def proj_copy(d):
        q = peer(d)
        return remote(psend.at[q], my_rows(blocks.at[1], p), pr_s.at[d], pr_r.at[d], member=q)

    def proj_send(d, carry):
        proj_copy(d).start()
        return carry

    lax.fori_loop(1, n, proj_send, 0)
    want_west.start()
    want_east.start()
    send_state((1, 2))
    blocks[1, pl.ds(pl.multiple_of(p * members, members), members), :] = psend[p]
    own = pltpu.make_async_copy(band(pv, p), my_rows(state, p), load_sem)
    own.start()

    def proj_wait(d, carry):
        proj_copy(d).wait_recv()
        return carry

    lax.fori_loop(1, n, proj_wait, 0)
    up = remote(blocks.at[1], blocks.at[0], halo_s.at[0], halo_r.at[0], member=peer(1))
    down = remote(blocks.at[1], blocks.at[2], halo_s.at[1], halo_r.at[1], member=peer(n - 1))
    up.start()
    down.start()
    send_state((3, 4, 5, 6, 7, 8))

    departs, precision = [None] * 3, [None] * 3

    def centre(j):
        values = blocks[j].astype(F32)
        ybar = jnp.mean(values, axis=0, keepdims=True)
        pert[:, 256 * j : 256 * (j + 1)] = (values - ybar).astype(BF16)
        k = lax.rem(p + n - 1 + j, n)
        departs[j] = pair(data, k) - ybar
        precision[j] = pair(data, n + k)

    centre(1)
    up.wait_recv()
    centre(0)
    down.wait_recv()
    centre(2)
    want_west.wait_recv()
    want_east.wait_recv()

    def weigh(asks):
        moments = []
        for j in range(3):
            code = asks[j : j + 1, :]
            w = jnp.where(code > 0.0, precision[j] * 2.0 / (1.0 + code), 0.0)
            cols = slice(256 * j, 256 * (j + 1))
            wp[:, cols] = (pert[:, cols].astype(F32) * w).astype(BF16)
            moments.append(w * departs[j])
        return row_dot(jnp.concatenate(moments, axis=1), pert[...], NT)

    def gram(i):
        return dot(wp[128 * i : 128 * (i + 1), :], pert[128 * i :, :], NT)

    def gram_copy(side, i, where):
        part = (pl.ds(128 * i, 128), pl.ds(128 * i, 512 - 128 * i))
        return remote(gs.at[side].at[part], gr.at[1 - side].at[part], g_s.at[side, i], g_r.at[1 - side, i], region=where)

    def moment_copy(side, where):
        return remote(vs.at[side], vr.at[1 - side], v_s.at[side], v_r.at[1 - side], region=where)

    for side_, where in ((0, west), (1, east)):
        moment = weigh(asked[side_])
        vs[side_] = jnp.broadcast_to(moment, (8, 512))
        moment_copy(side_, where).start()
        for i in range(4):
            gs[side_, 128 * i : 128 * (i + 1), 128 * i :] = gram(i).astype(BF16)
            gram_copy(side_, i, where).start()
    gvec = weigh(want[8:16, :])
    for i in range(4):
        amat[128 * i : 128 * (i + 1), 128 * i :] = gram(i)

    def eye(rows, cols, at):
        return iota((rows, cols), 0) + at == iota((rows, cols), 1)

    squares = jnp.zeros((1, 1), F32)
    for i in range(4):
        for side_, where in ((0, west), (1, east)):
            gram_copy(side_, i, where).wait_recv()
        rows, width = slice(128 * i, 128 * (i + 1)), 512 - 128 * i
        a = amat[rows, 128 * i :] + (gr[0, rows, 128 * i :].astype(F32) + gr[1, rows, 128 * i :].astype(F32))
        a = a + jnp.where(eye(128, width, 0), 511.0, 0.0)
        amat[rows, 128 * i :] = a
        twice = a * a * jnp.where(iota((1, width), 1) < 128, 1.0, 2.0)
        squares = squares + jnp.sum(jnp.sum(twice, axis=0, keepdims=True), axis=1, keepdims=True)
    norm = jnp.sqrt(squares)
    inverse = 1.0 / norm
    for i in range(4):
        rows = slice(128 * i, 128 * (i + 1))
        scaled = amat[rows, 128 * i :] * inverse
        z[0, rows, 128 * i :] = scaled.astype(BF16)
        for j in range(i + 1, 4):
            z[0, 128 * j : 128 * (j + 1), rows] = scaled[:, 128 * (j - i) : 128 * (j - i + 1)].T.astype(BF16)

    half = 256
    halves = [slice(0, half), slice(half, 512)]
    for k, rows in enumerate(halves):
        first = jnp.where(eye(half, 512, half * k), 1.5, 0.0) - 0.5 * z[0, rows, :].astype(F32)
        y[1, rows, :] = first.astype(BF16)
    for rows in halves:
        z[1, rows, :] = dot(y[1, rows, :], z[0]).astype(BF16)

    def make_t(now):
        for k, rows in enumerate(halves):
            product = dot(z[now, rows, :], y[now])
            t[rows, :] = (jnp.where(eye(half, 512, half * k), 1.5, 0.0) - 0.5 * product).astype(BF16)

    def step(it, carry):
        now = lax.rem(it, 2)
        make_t(now)
        for rows in halves:
            y[1 - now, rows, :] = dot(y[now, rows, :], t[...]).astype(BF16)
            z[1 - now, rows, :] = dot(t[rows, :], z[now]).astype(BF16)
        return carry

    lax.fori_loop(1, ITERS - 1, step, 0)
    last = (ITERS - 1) % 2
    make_t(last)
    yf = y.at[1 - last]
    for rows in halves:
        yf[rows, :] = dot(y[last, rows, :], t[...]).astype(BF16)

    def east_copy(d):
        q = peer(d)
        return remote(my_rows(yf, q), my_rows(ye, q), y_s.at[d], y_r.at[d], region=west)

    def east_send(d, carry):
        east_copy(d).start()
        return carry

    lax.fori_loop(0, n, east_send, 0)
    for side_, where in ((0, west), (1, east)):
        moment_copy(side_, where).wait_recv()
    gvec = gvec + (vr[0, 0:1, :] + vr[1, 0:1, :])
    root = jnp.sqrt(norm)
    wbar = row_dot(row_dot(gvec, yf[...], NT) / root, yf[...], NT) / root
    scale = jnp.sqrt(F32(511.0)) / root
    fs[...] = jnp.where(iota((8, 512), 0) == 0, wbar, jnp.broadcast_to(scale, (8, 512)))
    factors = remote(fs, fe, f_s, f_r, region=west)
    factors.start()

    own.wait()

    def state_wait(d, carry):
        state_copy(d).wait_recv()
        return carry

    lax.fori_loop(1, n, state_wait, 0)
    factors.wait_recv()
    sums, bases, owns, easts = [], [], [], []
    tile = 512
    wide = jnp.concatenate(
        [split_rows(wbar), split_rows(fe[0:1, :]), jnp.ones((16, 512), BF16)], axis=0
    )
    totals = [jnp.sum(w, axis=1, keepdims=True) for w in (wbar, fe[0:1, :])]
    for c in range(4):
        cols = slice(tile * c, tile * (c + 1))
        part = share[0, :, cols].astype(F32) * 0.125
        rows = dot(wide, state[:, cols])
        xbar = rows[32:33] * (1.0 / 512.0)
        shifts = [
            jnp.sum(rows[16 * k : 16 * (k + 1)], axis=0, keepdims=True) - totals[k] * xbar for k in range(2)
        ]
        sums.append(xbar)
        bases.append(xbar + (1.0 - part) * shifts[0] + part * shifts[1])
        owns.append((1.0 - part) * scale)
        easts.append(part * fe[1:2, 0:tile])

    def out_copy(d):
        q = peer(d)
        return remote(res.at[q], band(out, p), out_s.at[d], out_r.at[d], member=q)

    def update(q):
        at = pl.ds(pl.multiple_of(q * members, members), members)
        lhs = jnp.concatenate([yf[at, :], ye[at, :]], axis=0)
        weight = jnp.sum(lhs.astype(F32), axis=1, keepdims=True)
        for c in range(4):
            cols = slice(tile * c, tile * (c + 1))
            both = dot(lhs, state[:, cols]) - weight * sums[c]
            value = bases[c] + owns[c] * both[:members] + easts[c] * both[members:]
            res[q, :, cols] = value.astype(BF16)

    def update_one(d, carry):
        east_copy(d).wait_recv()
        update(peer(d))
        out_copy(d).start()
        return carry

    lax.fori_loop(1, n, update_one, 0)
    east_copy(0).wait_recv()
    update(p)
    mine = pltpu.make_async_copy(res.at[p], band(out, p), load_sem)
    mine.start()

    def finish(d, carry):
        out_copy(d).wait()
        state_copy(d).wait_send()
        proj_copy(d).wait_send()
        east_copy(d).wait_send()
        return carry

    lax.fori_loop(1, n, finish, 0)
    east_copy(0).wait_send()
    mine.wait()
    for c in (want_west, want_east, up, down, factors):
        c.wait_send()
    for side_, where in ((0, west), (1, east)):
        moment_copy(side_, where).wait_send()
        for i in range(4):
            gram_copy(side_, i, where).wait_send()


def local(n, regions, prior, values, precision, line, lookup, count, dist, share):
    dma = pltpu.SemaphoreType.DMA
    hbm = pl.BlockSpec(memory_space=pltpu.HBM)
    members = prior.shape[0]
    return pl.pallas_call(
        functools.partial(kernel, n, regions),
        out_shape=jax.ShapeDtypeStruct(prior.shape, BF16),
        in_specs=[hbm] * 7 + [pl.BlockSpec(memory_space=pltpu.SMEM)],
        out_specs=pl.BlockSpec(memory_space=pl.ANY),
        scratch_shapes=[
            pltpu.VMEM((32, 128), jnp.int32),
            pltpu.VMEM((32, 128), BF16),
            pltpu.VMEM((32, 128), BF16),
            pltpu.VMEM((64, 128), F32),
            pltpu.VMEM(lookup.shape, jnp.int32),
            pltpu.VMEM(dist.shape, jnp.int32),
            pltpu.VMEM(share.shape, jnp.int32),
            pltpu.VMEM(prior.shape, BF16),
            pltpu.VMEM((512, 2048), BF16),
            pltpu.VMEM((n, members, 256), BF16),
            pltpu.VMEM((3, 512, 256), BF16),
            pltpu.VMEM((512, 768), BF16),
            pltpu.VMEM((512, 768), BF16),
            pltpu.VMEM((32, 256), F32),
            pltpu.VMEM((2, 8, 256), F32),
            pltpu.VMEM((2, 512, 512), BF16),
            pltpu.VMEM((2, 512, 512), BF16),
            pltpu.VMEM((2, 8, 512), F32),
            pltpu.VMEM((2, 8, 512), F32),
            pltpu.VMEM((512, 512), F32),
            pltpu.VMEM((2, 512, 512), BF16),
            pltpu.VMEM((2, 512, 512), BF16),
            pltpu.VMEM((512, 512), BF16),
            pltpu.VMEM((512, 512), BF16),
            pltpu.VMEM((8, 512), F32),
            pltpu.VMEM((8, 512), F32),
            pltpu.VMEM((n, members, 2048), BF16),
            dma, dma((6,)),
            dma((n,)), dma((n,)),
            dma((n,)), dma((n,)),
            dma((2,)), dma((2,)),
            dma((2,)), dma((2,)),
            dma((2, 4)), dma((2, 4)),
            dma((2,)), dma((2,)),
            dma((n,)), dma((n,)),
            dma, dma,
            dma((n,)), dma((n,)),
        ],
        compiler_params=pltpu.CompilerParams(
            collective_id=0, has_side_effects=True, vmem_limit_bytes=63 * 1024 * 1024
        ),
    )(prior, *(a.reshape(-1, 128) for a in (line, values, precision)), lookup, dist, share, count)


def solution(mesh):
    in_specs = (
        P("member", "region"),
        P("region"),
        P("region"),
        P("region"),
        P("region", None, None),
        P("region", "member"),
        P("region", "member", None),
        P("region", "member", None),
    )
    body = functools.partial(local, mesh.shape["member"], mesh.shape["region"])
    return jax.shard_map(body, mesh=mesh, in_specs=in_specs, out_specs=P("member", "region"), check_vma=False)
```

```python
import functools

import jax
import jax.numpy as jnp
from jax import lax
from jax.experimental import pallas as pl
from jax.experimental.pallas import tpu as pltpu
from jax.sharding import PartitionSpec as P

ITERS = 6
MESH = pl.DeviceIdType.MESH
F32 = jnp.float32
BF16 = jnp.bfloat16
NN = (((1,), (0,)), ((), ()))
NT = (((1,), (1,)), ((), ()))


def dot(a, b, dims=NN):
    return lax.dot_general(a, b, dims, preferred_element_type=F32)


def iota(shape, dim):
    return lax.broadcasted_iota(jnp.int32, shape, dim)


def split_rows(x):
    hi = x.astype(BF16).astype(F32)
    mid = (x - hi).astype(BF16).astype(F32)
    low = x - hi - mid
    row = iota((16, x.shape[1]), 0)
    rows = jnp.where(row == 0, hi, jnp.where(row == 1, mid, jnp.where(row == 2, low, 0.0)))
    return rows.astype(BF16)


def row_dot(x, b, dims):
    return jnp.sum(dot(split_rows(x), b, dims), axis=0, keepdims=True)


def kernel(
    n, regions,
    prior, line_in, values_in, precision_in, lookup_in, dist_in, share_in, count,
    out,
    line, values, precisions, data, lookup, dist, share, pv, state, psend, blocks, pert, wp, want, asked, gs, gr, vs, vr, amat, y, z, t, ye, fs, fe, res,
    load_sem, small_sem, own_sem, in_s, in_r, pr_s, pr_r, halo_s, halo_r, want_s, want_r, g_s, g_r, v_s, v_r, y_s, y_r, f_s, f_r, out_s, out_r,
):
    p = lax.axis_index("member")
    s = lax.axis_index("region")
    members = 512 // n
    west, east = lax.rem(s + regions - 1, regions), lax.rem(s + 1, regions)

    def remote(src, dst, ss, rs, **where):
        return pltpu.make_async_remote_copy(
            src_ref=src, dst_ref=dst, send_sem=ss, recv_sem=rs, device_id=where, device_id_type=MESH
        )

    def peer(d):
        return lax.rem(p + d, n)

    def nth(i):
        k = n // 2 - lax.div(i + 1, 2)
        return jnp.where(lax.rem(i, 2) == 1, k, n - k)

    def my_rows(ref, k):
        return ref.at[pl.ds(pl.multiple_of(k * members, members), members)]

    def half_band(ref, k, h):
        return ref.at[:, pl.ds(pl.multiple_of(k * 2048 + 1024 * h, 1024), 1024)]

    barrier = pltpu.get_barrier_semaphore()

    def greet(d, carry):
        pl.semaphore_signal(barrier, inc=1, device_id={"member": peer(d)}, device_id_type=MESH)
        return carry

    lax.fori_loop(1, n, greet, 0)
    for other in (west, east):
        pl.semaphore_signal(barrier, inc=1, device_id={"region": other}, device_id_type=MESH)

    load = pltpu.make_async_copy(prior, pv, load_sem)
    load.start()
    smalls = [
        pltpu.make_async_copy(src, dst, small_sem.at[k])
        for k, (src, dst) in enumerate(
            (
                (line_in, line),
                (lookup_in, lookup),
                (dist_in, dist),
                (values_in, values),
                (precision_in, precisions),
                (share_in, share),
            )
        )
    ]
    for c in smalls:
        c.start()
    def pair(ref, k):
        return jnp.concatenate([ref[pl.ds(2 * k, 1), :], ref[pl.ds(2 * k + 1, 1), :]], axis=1)

    def project(q):
        rows = [pv[:, pl.ds(pl.multiple_of(q * 2048 + 256 * h, 256), 256)] for h in range(8)]
        at = pair(line, q)
        pick = jnp.where(iota((256, 256), 0) == (at & 255), 1.0, 0.0).astype(BF16)
        found = dot(jnp.concatenate(rows, axis=0), pick)
        high = lax.shift_right_logical(at, 8) & 7
        total = jnp.zeros((members, 256), F32)
        for h in range(8):
            total = total + jnp.where(high == h, found[members * h : members * (h + 1)], 0.0)
        return total.astype(BF16)

    smalls[0].wait()
    load.wait()

    def project_one(q, carry):
        psend[q] = project(q)
        return carry

    lax.fori_loop(0, n, project_one, 0)
    pl.semaphore_wait(barrier, n + 1)

    def state_copy(d, h):
        q = peer(d)
        return remote(half_band(pv, q, h), my_rows(state.at[h], p), in_s.at[h, d], in_r.at[h, d], member=q)

    def send_state(h, pairs):
        for k in pairs:
            state_copy(k, h).start()
            if 2 * k != n:
                state_copy(n - k, h).start()

    want_west = remote(want.at[pl.ds(0, 8)], asked.at[1], want_s.at[0], want_r.at[1], region=west)
    want_east = remote(want.at[pl.ds(16, 8)], asked.at[0], want_s.at[1], want_r.at[0], region=east)

    def proj_copy(d):
        q = peer(d)
        return remote(psend.at[q], my_rows(blocks.at[1], p), pr_s.at[d], pr_r.at[d], member=q)

    def proj_send(d, carry):
        proj_copy(d).start()
        return carry

    lax.fori_loop(1, n, proj_send, 0)
    send_state(0, range(1, 4))
    blocks[1, pl.ds(pl.multiple_of(p * members, members), members), :] = psend[p]
    owns = [
        pltpu.make_async_copy(half_band(pv, p, h), my_rows(state.at[h], p), own_sem.at[h]) for h in range(2)
    ]
    for c in owns:
        c.start()

    for c in smalls[1:]:
        c.wait()
    data[0:32, :] = values[...].astype(F32)
    data[32:64, :] = precisions[...].astype(F32)

    slots = lookup.shape[-1]
    named = lookup[0, pl.ds(p, 1), :]
    side = lax.shift_right_logical(named, 12)
    offset = (lax.shift_right_logical(named, 8) & 15) - p + 1
    live = iota((1, slots), 1) < count[0, 0]
    code = jnp.where(live, (dist[0] + 1).astype(F32), 0.0)
    group = jnp.where(iota((32, slots), 0) == side * 8 + offset, code, 0.0).astype(BF16)
    place = jnp.where(iota((256, slots), 0) == (named & 255), 1.0, 0.0).astype(BF16)
    want[...] = dot(group, place, NT)

    want_west.start()
    want_east.start()

    def proj_wait(d, carry):
        proj_copy(d).wait_recv()
        return carry

    lax.fori_loop(1, n, proj_wait, 0)
    up = remote(blocks.at[1], blocks.at[0], halo_s.at[0], halo_r.at[0], member=peer(1))
    down = remote(blocks.at[1], blocks.at[2], halo_s.at[1], halo_r.at[1], member=peer(n - 1))
    up.start()
    down.start()
    send_state(0, range(n // 2, 3, -1))
    send_state(1, range(n // 2, 0, -1))

    departs, precision = [None] * 3, [None] * 3

    def centre(j):
        values = blocks[j].astype(F32)
        ybar = jnp.mean(values, axis=0, keepdims=True)
        pert[:, 256 * j : 256 * (j + 1)] = (values - ybar).astype(BF16)
        k = lax.rem(p + n - 1 + j, n)
        departs[j] = pair(data, k) - ybar
        precision[j] = pair(data, n + k)

    centre(1)
    up.wait_recv()
    centre(0)
    down.wait_recv()
    centre(2)
    want_west.wait_recv()
    want_east.wait_recv()

    def weigh(asks):
        moments = []
        for j in range(3):
            code = asks[j : j + 1, :]
            w = jnp.where(code > 0.0, precision[j] * 2.0 / (1.0 + code), 0.0)
            cols = slice(256 * j, 256 * (j + 1))
            wp[:, cols] = (pert[:, cols].astype(F32) * w).astype(BF16)
            moments.append(w * departs[j])
        return row_dot(jnp.concatenate(moments, axis=1), pert[...], NT)

    def gram(i):
        return dot(wp[128 * i : 128 * (i + 1), :], pert[128 * i :, :], NT)

    def gram_copy(side, i, where):
        part = (pl.ds(128 * i, 128), pl.ds(128 * i, 512 - 128 * i))
        return remote(gs.at[side].at[part], gr.at[1 - side].at[part], g_s.at[side, i], g_r.at[1 - side, i], region=where)

    def moment_copy(side, where):
        return remote(vs.at[side], vr.at[1 - side], v_s.at[side], v_r.at[1 - side], region=where)

    for side_, where in ((0, west), (1, east)):
        moment = weigh(asked[side_])
        vs[side_] = jnp.broadcast_to(moment, (8, 512))
        moment_copy(side_, where).start()
        for i in range(4):
            gs[side_, 128 * i : 128 * (i + 1), 128 * i :] = gram(i).astype(BF16)
            gram_copy(side_, i, where).start()
    gvec = weigh(want[8:16, :])
    for i in range(4):
        amat[128 * i : 128 * (i + 1), 128 * i :] = gram(i)

    def eye(rows, cols, at):
        return iota((rows, cols), 0) + at == iota((rows, cols), 1)

    squares = jnp.zeros((1, 1), F32)
    for i in range(4):
        for side_, where in ((0, west), (1, east)):
            gram_copy(side_, i, where).wait_recv()
        rows, width = slice(128 * i, 128 * (i + 1)), 512 - 128 * i
        a = amat[rows, 128 * i :] + (gr[0, rows, 128 * i :].astype(F32) + gr[1, rows, 128 * i :].astype(F32))
        a = a + jnp.where(eye(128, width, 0), 511.0, 0.0)
        amat[rows, 128 * i :] = a
        twice = a * a * jnp.where(iota((1, width), 1) < 128, 1.0, 2.0)
        squares = squares + jnp.sum(jnp.sum(twice, axis=0, keepdims=True), axis=1, keepdims=True)
    norm = jnp.sqrt(squares)
    inverse = 1.0 / norm
    for i in range(4):
        rows = slice(128 * i, 128 * (i + 1))
        scaled = amat[rows, 128 * i :] * inverse
        z[0, rows, 128 * i :] = scaled.astype(BF16)
        for j in range(i + 1, 4):
            z[0, 128 * j : 128 * (j + 1), rows] = scaled[:, 128 * (j - i) : 128 * (j - i + 1)].T.astype(BF16)

    half = 256
    halves = [slice(0, half), slice(half, 512)]
    for k, rows in enumerate(halves):
        first = jnp.where(eye(half, 512, half * k), 1.5, 0.0) - 0.5 * z[0, rows, :].astype(F32)
        y[1, rows, :] = first.astype(BF16)
    for rows in halves:
        z[1, rows, :] = dot(y[1, rows, :], z[0]).astype(BF16)

    def make_t(now):
        for k, rows in enumerate(halves):
            product = dot(z[now, rows, :], y[now])
            t[rows, :] = (jnp.where(eye(half, 512, half * k), 1.5, 0.0) - 0.5 * product).astype(BF16)

    def step(it, carry):
        now = lax.rem(it, 2)
        make_t(now)
        for rows in halves:
            y[1 - now, rows, :] = dot(y[now, rows, :], t[...]).astype(BF16)
            z[1 - now, rows, :] = dot(t[rows, :], z[now]).astype(BF16)
        return carry

    lax.fori_loop(1, ITERS - 1, step, 0)
    last = (ITERS - 1) % 2
    make_t(last)
    yf = y.at[1 - last]
    for rows in halves:
        yf[rows, :] = dot(y[last, rows, :], t[...]).astype(BF16)

    def east_copy(d):
        q = peer(d)
        return remote(my_rows(yf, q), my_rows(ye, q), y_s.at[d], y_r.at[d], region=west)

    def east_send(i, carry):
        east_copy(nth(i)).start()
        return carry

    lax.fori_loop(0, n - 1, east_send, 0)
    east_copy(0).start()
    for side_, where in ((0, west), (1, east)):
        moment_copy(side_, where).wait_recv()
    gvec = gvec + (vr[0, 0:1, :] + vr[1, 0:1, :])
    root = jnp.sqrt(norm)
    wbar = row_dot(row_dot(gvec, yf[...], NT) / root, yf[...], NT) / root
    scale = jnp.sqrt(F32(511.0)) / root
    fs[...] = jnp.where(iota((8, 512), 0) == 0, wbar, jnp.broadcast_to(scale, (8, 512)))
    factors = remote(fs, fe, f_s, f_r, region=west)
    factors.start()

    factors.wait_recv()
    tile = 512
    wide = jnp.concatenate(
        [split_rows(wbar), split_rows(fe[0:1, :]), jnp.ones((16, 512), BF16)], axis=0
    )
    totals = [jnp.sum(w, axis=1, keepdims=True) for w in (wbar, fe[0:1, :])]

    def out_copy(d, h):
        q = peer(d)
        return remote(res.at[h, q], half_band(out, p, h), out_s.at[h, d], out_r.at[h, d], member=q)

    mine = []
    for h in range(2):
        owns[h].wait()

        def state_wait(d, carry):
            state_copy(d, h).wait_recv()
            return carry

        lax.fori_loop(1, n, state_wait, 0)
        rules = []
        for c in range(2):
            cols = slice(tile * c, tile * (c + 1))
            part = share[0, :, 1024 * h + tile * c : 1024 * h + tile * (c + 1)].astype(F32) * 0.125
            rows = dot(wide, state[h, :, cols])
            xbar = rows[32:33] * (1.0 / 512.0)
            shifts = [
                jnp.sum(rows[16 * k : 16 * (k + 1)], axis=0, keepdims=True) - totals[k] * xbar
                for k in range(2)
            ]
            base = xbar + (1.0 - part) * shifts[0] + part * shifts[1]
            rules.append((cols, xbar, base, (1.0 - part) * scale, part * fe[1:2, 0:tile]))

        def update(q):
            at = pl.ds(pl.multiple_of(q * members, members), members)
            lhs = jnp.concatenate([yf[at, :], ye[at, :]], axis=0)
            weight = jnp.sum(lhs.astype(F32), axis=1, keepdims=True)
            for cols, xbar, base, here, there in rules:
                both = dot(lhs, state[h, :, cols]) - weight * xbar
                res[h, q, :, cols] = (base + here * both[:members] + there * both[members:]).astype(BF16)

        def update_one(i, carry):
            d = nth(i)
            if h == 0:
                east_copy(d).wait_recv()
            update(peer(d))
            out_copy(d, h).start()
            return carry

        lax.fori_loop(0, n - 1, update_one, 0)
        if h == 0:
            east_copy(0).wait_recv()
        update(p)
        mine.append(pltpu.make_async_copy(res.at[h, p], half_band(out, p, h), own_sem.at[h]))
        mine[h].start()

    def finish(d, carry):
        for h in range(2):
            out_copy(d, h).wait()
            state_copy(d, h).wait_send()
        proj_copy(d).wait_send()
        east_copy(d).wait_send()
        return carry

    lax.fori_loop(1, n, finish, 0)
    east_copy(0).wait_send()
    for c in mine:
        c.wait()
    for c in (want_west, want_east, up, down, factors):
        c.wait_send()
    for side_, where in ((0, west), (1, east)):
        moment_copy(side_, where).wait_send()
        for i in range(4):
            gram_copy(side_, i, where).wait_send()


def local(n, regions, prior, values, precision, line, lookup, count, dist, share):
    dma = pltpu.SemaphoreType.DMA
    hbm = pl.BlockSpec(memory_space=pltpu.HBM)
    members = prior.shape[0]
    return pl.pallas_call(
        functools.partial(kernel, n, regions),
        out_shape=pltpu.VMEM(prior.shape, BF16),
        in_specs=[hbm] * 7 + [pl.BlockSpec(memory_space=pltpu.SMEM)],
        out_specs=pl.BlockSpec(memory_space=pl.ANY),
        scratch_shapes=[
            pltpu.VMEM((32, 128), jnp.int32),
            pltpu.VMEM((32, 128), BF16),
            pltpu.VMEM((32, 128), BF16),
            pltpu.VMEM((64, 128), F32),
            pltpu.VMEM(lookup.shape, jnp.int32),
            pltpu.VMEM(dist.shape, jnp.int32),
            pltpu.VMEM(share.shape, jnp.int32),
            pltpu.VMEM(prior.shape, BF16),
            pltpu.VMEM((2, 512, 1024), BF16),
            pltpu.VMEM((n, members, 256), BF16),
            pltpu.VMEM((3, 512, 256), BF16),
            pltpu.VMEM((512, 768), BF16),
            pltpu.VMEM((512, 768), BF16),
            pltpu.VMEM((32, 256), F32),
            pltpu.VMEM((2, 8, 256), F32),
            pltpu.VMEM((2, 512, 512), BF16),
            pltpu.VMEM((2, 512, 512), BF16),
            pltpu.VMEM((2, 8, 512), F32),
            pltpu.VMEM((2, 8, 512), F32),
            pltpu.VMEM((512, 512), F32),
            pltpu.VMEM((2, 512, 512), BF16),
            pltpu.VMEM((2, 512, 512), BF16),
            pltpu.VMEM((512, 512), BF16),
            pltpu.VMEM((512, 512), BF16),
            pltpu.VMEM((8, 512), F32),
            pltpu.VMEM((8, 512), F32),
            pltpu.VMEM((2, n, members, 1024), BF16),
            dma, dma((6,)), dma((2,)),
            dma((2, n)), dma((2, n)),
            dma((n,)), dma((n,)),
            dma((2,)), dma((2,)),
            dma((2,)), dma((2,)),
            dma((2, 4)), dma((2, 4)),
            dma((2,)), dma((2,)),
            dma((n,)), dma((n,)),
            dma, dma,
            dma((2, n)), dma((2, n)),
        ],
        compiler_params=pltpu.CompilerParams(
            collective_id=0, has_side_effects=True, vmem_limit_bytes=60 * 1024 * 1024
        ),
    )(prior, *(a.reshape(-1, 128) for a in (line, values, precision)), lookup, dist, share, count)


def solution(mesh):
    in_specs = (
        P("member", "region"),
        P("region"),
        P("region"),
        P("region"),
        P("region", None, None),
        P("region", "member"),
        P("region", "member", None),
        P("region", "member", None),
    )
    body = functools.partial(local, mesh.shape["member"], mesh.shape["region"])
    return jax.shard_map(body, mesh=mesh, in_specs=in_specs, out_specs=P("member", "region"), check_vma=False)
```

```python
import functools

import jax
import jax.numpy as jnp
from jax import lax
from jax.experimental import pallas as pl
from jax.experimental.pallas import tpu as pltpu
from jax.sharding import PartitionSpec as P

ITERS = 6
MESH = pl.DeviceIdType.MESH
F32 = jnp.float32
BF16 = jnp.bfloat16
NN = (((1,), (0,)), ((), ()))
NT = (((1,), (1,)), ((), ()))


def dot(a, b, dims=NN):
    return lax.dot_general(a, b, dims, preferred_element_type=F32)


def iota(shape, dim):
    return lax.broadcasted_iota(jnp.int32, shape, dim)


def split_rows(x):
    hi = x.astype(BF16).astype(F32)
    mid = (x - hi).astype(BF16).astype(F32)
    low = x - hi - mid
    row = iota((16, x.shape[1]), 0)
    rows = jnp.where(row == 0, hi, jnp.where(row == 1, mid, jnp.where(row == 2, low, 0.0)))
    return rows.astype(BF16)


def row_dot(x, b, dims):
    return jnp.sum(dot(split_rows(x), b, dims), axis=0, keepdims=True)


def kernel(
    n, regions,
    prior, line_in, values_in, precision_in, lookup_in, dist_in, share_in, count,
    out,
    line, values, precisions, data, lookup, dist, share, pv, state, psend, blocks, pert, wp, want, asked, gs, gr, vs, vr, amat, y, z, t, ye, fs, fe, res,
    load_sem, small_sem, own_sem, in_s, in_r, pr_s, pr_r, halo_s, halo_r, want_s, want_r, g_s, g_r, v_s, v_r, y_s, y_r, f_s, f_r, out_s, out_r,
):
    p = lax.axis_index("member")
    s = lax.axis_index("region")
    members = 512 // n
    west, east = lax.rem(s + regions - 1, regions), lax.rem(s + 1, regions)

    def remote(src, dst, ss, rs, **where):
        return pltpu.make_async_remote_copy(
            src_ref=src, dst_ref=dst, send_sem=ss, recv_sem=rs, device_id=where, device_id_type=MESH
        )

    def peer(d):
        return lax.rem(p + d, n)

    def nth(i):
        k = n // 2 - lax.div(i + 1, 2)
        return jnp.where(lax.rem(i, 2) == 1, k, n - k)

    def my_rows(ref, k):
        return ref.at[pl.ds(pl.multiple_of(k * members, members), members)]

    def half_band(ref, k, h):
        return ref.at[:, pl.ds(pl.multiple_of(k * 2048 + 1024 * h, 1024), 1024)]

    barrier = pltpu.get_barrier_semaphore()

    def greet(d, carry):
        pl.semaphore_signal(barrier, inc=1, device_id={"member": peer(d)}, device_id_type=MESH)
        return carry

    lax.fori_loop(1, n, greet, 0)
    for other in (west, east):
        pl.semaphore_signal(barrier, inc=1, device_id={"region": other}, device_id_type=MESH)

    load = pltpu.make_async_copy(prior, pv, load_sem)
    load.start()
    smalls = [
        pltpu.make_async_copy(src, dst, small_sem.at[k])
        for k, (src, dst) in enumerate(
            (
                (line_in, line),
                (lookup_in, lookup),
                (dist_in, dist),
                (values_in, values),
                (precision_in, precisions),
                (share_in, share),
            )
        )
    ]
    for c in smalls:
        c.start()
    def pair(ref, k):
        return jnp.concatenate([ref[pl.ds(2 * k, 1), :], ref[pl.ds(2 * k + 1, 1), :]], axis=1)

    def project(q):
        rows = [pv[:, pl.ds(pl.multiple_of(q * 2048 + 256 * h, 256), 256)] for h in range(8)]
        at = pair(line, q)
        pick = jnp.where(iota((256, 256), 0) == (at & 255), 1.0, 0.0).astype(BF16)
        found = dot(jnp.concatenate(rows, axis=0), pick)
        high = lax.shift_right_logical(at, 8) & 7
        total = jnp.zeros((members, 256), F32)
        for h in range(8):
            total = total + jnp.where(high == h, found[members * h : members * (h + 1)], 0.0)
        return total.astype(BF16)

    smalls[0].wait()
    load.wait()

    def project_one(q, carry):
        psend[q] = project(q)
        return carry

    lax.fori_loop(0, n, project_one, 0)
    pl.semaphore_wait(barrier, n + 1)

    def state_copy(d, h):
        q = peer(d)
        return remote(half_band(pv, q, h), my_rows(state.at[h], p), in_s.at[h, d], in_r.at[h, d], member=q)

    def send_state(h, pairs):
        for k in pairs:
            state_copy(k, h).start()
            if 2 * k != n:
                state_copy(n - k, h).start()

    want_west = remote(want.at[pl.ds(0, 8)], asked.at[1], want_s.at[0], want_r.at[1], region=west)
    want_east = remote(want.at[pl.ds(16, 8)], asked.at[0], want_s.at[1], want_r.at[0], region=east)

    def proj_copy(d):
        q = peer(d)
        return remote(psend.at[q], my_rows(blocks.at[1], p), pr_s.at[d], pr_r.at[d], member=q)

    def proj_send(d, carry):
        proj_copy(d).start()
        return carry

    lax.fori_loop(1, n, proj_send, 0)
    send_state(0, range(1, 4))
    blocks[1, pl.ds(pl.multiple_of(p * members, members), members), :] = psend[p]
    owns = [
        pltpu.make_async_copy(half_band(pv, p, h), my_rows(state.at[h], p), own_sem.at[h]) for h in range(2)
    ]
    for c in owns:
        c.start()

    for c in smalls[1:]:
        c.wait()
    data[0:32, :] = values[...].astype(F32)
    data[32:64, :] = precisions[...].astype(F32)

    slots = lookup.shape[-1]
    named = lookup[0, pl.ds(p, 1), :]
    side = lax.shift_right_logical(named, 12)
    offset = (lax.shift_right_logical(named, 8) & 15) - p + 1
    live = iota((1, slots), 1) < count[0, 0]
    code = jnp.where(live, (dist[0] + 1).astype(F32), 0.0)
    group = jnp.where(iota((32, slots), 0) == side * 8 + offset, code, 0.0).astype(BF16)
    place = jnp.where(iota((256, slots), 0) == (named & 255), 1.0, 0.0).astype(BF16)
    want[...] = dot(group, place, NT)

    want_west.start()
    want_east.start()

    def proj_wait(d, carry):
        proj_copy(d).wait_recv()
        return carry

    lax.fori_loop(1, n, proj_wait, 0)
    up = remote(blocks.at[1], blocks.at[0], halo_s.at[0], halo_r.at[0], member=peer(1))
    down = remote(blocks.at[1], blocks.at[2], halo_s.at[1], halo_r.at[1], member=peer(n - 1))
    up.start()
    down.start()
    send_state(0, range(n // 2, 3, -1))
    send_state(1, range(n // 2, 0, -1))

    departs, precision = [None] * 3, [None] * 3

    def centre(j):
        values = blocks[j].astype(F32)
        ybar = jnp.mean(values, axis=0, keepdims=True)
        pert[:, 256 * j : 256 * (j + 1)] = (values - ybar).astype(BF16)
        k = lax.rem(p + n - 1 + j, n)
        departs[j] = pair(data, k) - ybar
        precision[j] = pair(data, n + k)

    centre(1)
    up.wait_recv()
    centre(0)
    down.wait_recv()
    centre(2)
    want_west.wait_recv()
    want_east.wait_recv()

    def weigh(asks):
        moments = []
        for j in range(3):
            code = asks[j : j + 1, :]
            w = jnp.where(code > 0.0, precision[j] * 2.0 / (1.0 + code), 0.0)
            cols = slice(256 * j, 256 * (j + 1))
            wp[:, cols] = (pert[:, cols].astype(F32) * w).astype(BF16)
            moments.append(w * departs[j])
        return row_dot(jnp.concatenate(moments, axis=1), pert[...], NT)

    def gram(i):
        return dot(wp[128 * i : 128 * (i + 1), :], pert[128 * i :, :], NT)

    def gram_copy(side, i, where):
        part = (pl.ds(128 * i, 128), pl.ds(128 * i, 512 - 128 * i))
        return remote(gs.at[side].at[part], gr.at[1 - side].at[part], g_s.at[side, i], g_r.at[1 - side, i], region=where)

    def moment_copy(side, where):
        return remote(vs.at[side], vr.at[1 - side], v_s.at[side], v_r.at[1 - side], region=where)

    for side_, where in ((0, west), (1, east)):
        moment = weigh(asked[side_])
        vs[side_] = jnp.broadcast_to(moment, (8, 512))
        moment_copy(side_, where).start()
        for i in range(4):
            gs[side_, 128 * i : 128 * (i + 1), 128 * i :] = gram(i).astype(BF16)
            gram_copy(side_, i, where).start()
    gvec = weigh(want[8:16, :])
    for i in range(4):
        amat[128 * i : 128 * (i + 1), 128 * i :] = gram(i)

    def eye(rows, cols, at):
        return iota((rows, cols), 0) + at == iota((rows, cols), 1)

    squares = jnp.zeros((1, 1), F32)
    for i in range(4):
        for side_, where in ((0, west), (1, east)):
            gram_copy(side_, i, where).wait_recv()
        rows, width = slice(128 * i, 128 * (i + 1)), 512 - 128 * i
        a = amat[rows, 128 * i :] + (gr[0, rows, 128 * i :].astype(F32) + gr[1, rows, 128 * i :].astype(F32))
        a = a + jnp.where(eye(128, width, 0), 511.0, 0.0)
        amat[rows, 128 * i :] = a
        twice = a * a * jnp.where(iota((1, width), 1) < 128, 1.0, 2.0)
        squares = squares + jnp.sum(jnp.sum(twice, axis=0, keepdims=True), axis=1, keepdims=True)
    norm = jnp.sqrt(squares)
    inverse = 1.0 / norm
    for i in range(4):
        rows = slice(128 * i, 128 * (i + 1))
        scaled = amat[rows, 128 * i :] * inverse
        z[0, rows, 128 * i :] = scaled.astype(BF16)
        for j in range(i + 1, 4):
            z[0, 128 * j : 128 * (j + 1), rows] = scaled[:, 128 * (j - i) : 128 * (j - i + 1)].T.astype(BF16)

    half = 256
    halves = [slice(0, half), slice(half, 512)]
    for k, rows in enumerate(halves):
        first = jnp.where(eye(half, 512, half * k), 1.5, 0.0) - 0.5 * z[0, rows, :].astype(F32)
        y[1, rows, :] = first.astype(BF16)
    for rows in halves:
        z[1, rows, :] = dot(y[1, rows, :], z[0]).astype(BF16)

    def make_t(now):
        for k, rows in enumerate(halves):
            product = dot(z[now, rows, :], y[now])
            t[rows, :] = (jnp.where(eye(half, 512, half * k), 1.5, 0.0) - 0.5 * product).astype(BF16)

    def step(it, carry):
        now = lax.rem(it, 2)
        make_t(now)
        for rows in halves:
            y[1 - now, rows, :] = dot(y[now, rows, :], t[...]).astype(BF16)
            z[1 - now, rows, :] = dot(t[rows, :], z[now]).astype(BF16)
        return carry

    lax.fori_loop(1, ITERS - 1, step, 0)
    last = (ITERS - 1) % 2
    make_t(last)
    yf = y.at[1 - last]
    for rows in halves:
        yf[rows, :] = dot(y[last, rows, :], t[...]).astype(BF16)

    def east_copy(d):
        q = peer(d)
        return remote(my_rows(yf, q), my_rows(ye, q), y_s.at[d], y_r.at[d], region=west)

    def east_send(i, carry):
        east_copy(nth(i)).start()
        return carry

    lax.fori_loop(0, n - 1, east_send, 0)
    east_copy(0).start()
    for side_, where in ((0, west), (1, east)):
        moment_copy(side_, where).wait_recv()
    gvec = gvec + (vr[0, 0:1, :] + vr[1, 0:1, :])
    root = jnp.sqrt(norm)
    wbar = row_dot(row_dot(gvec, yf[...], NT) / root, yf[...], NT) / root
    scale = jnp.sqrt(F32(511.0)) / root
    fs[...] = jnp.where(iota((8, 512), 0) == 0, wbar, jnp.broadcast_to(scale, (8, 512)))
    factors = remote(fs, fe, f_s, f_r, region=west)
    factors.start()

    factors.wait_recv()
    tile = 512
    wide = jnp.concatenate(
        [split_rows(wbar), split_rows(fe[0:1, :]), jnp.ones((16, 512), BF16)], axis=0
    )
    totals = [jnp.sum(w, axis=1, keepdims=True) for w in (wbar, fe[0:1, :])]

    def out_copy(d, h):
        q = peer(d)
        return remote(res.at[h, q], half_band(out, p, h), out_s.at[h, d], out_r.at[h, d], member=q)

    mine = []
    for h in range(2):
        owns[h].wait()

        def state_wait(d, carry):
            state_copy(d, h).wait_recv()
            return carry

        lax.fori_loop(1, n, state_wait, 0)
        rules = []
        for c in range(2):
            cols = slice(tile * c, tile * (c + 1))
            part = share[0, :, 1024 * h + tile * c : 1024 * h + tile * (c + 1)].astype(F32) * 0.125
            rows = dot(wide, state[h, :, cols])
            xbar = rows[32:33] * (1.0 / 512.0)
            shifts = [
                jnp.sum(rows[16 * k : 16 * (k + 1)], axis=0, keepdims=True) - totals[k] * xbar
                for k in range(2)
            ]
            base = xbar + (1.0 - part) * shifts[0] + part * shifts[1]
            rules.append((cols, xbar, base, (1.0 - part) * scale, part * fe[1:2, 0:tile]))

        def update(q):
            at = pl.ds(pl.multiple_of(q * members, members), members)
            lhs = jnp.concatenate([yf[at, :], ye[at, :]], axis=0)
            weight = jnp.sum(lhs.astype(F32), axis=1, keepdims=True)
            for cols, xbar, base, here, there in rules:
                both = dot(lhs, state[h, :, cols]) - weight * xbar
                res[h, q, :, cols] = (base + here * both[:members] + there * both[members:]).astype(BF16)

        def update_one(i, carry):
            d = nth(i)
            if h == 0:
                east_copy(d).wait_recv()
            update(peer(d))
            out_copy(d, h).start()
            return carry

        lax.fori_loop(0, n - 1, update_one, 0)
        if h == 0:
            east_copy(0).wait_recv()
        update(p)
        mine.append(pltpu.make_async_copy(res.at[h, p], half_band(out, p, h), own_sem.at[h]))
        mine[h].start()

    def settle(d, carry):
        proj_copy(d).wait_send()
        east_copy(d).wait_send()
        for h in range(2):
            state_copy(d, h).wait_send()
        return carry

    lax.fori_loop(1, n, settle, 0)
    east_copy(0).wait_send()
    for c in (want_west, want_east, up, down, factors):
        c.wait_send()
    for side_, where in ((0, west), (1, east)):
        moment_copy(side_, where).wait_send()
        for i in range(4):
            gram_copy(side_, i, where).wait_send()
    for c in mine:
        c.wait()

    def leave(i, carry):
        for h in range(2):
            out_copy(nth(i), h).wait_send()
        out_copy(nth(i), 0).wait_recv()
        return carry

    def arrive(i, carry):
        out_copy(nth(i), 1).wait_recv()
        return carry

    lax.fori_loop(0, n - 1, leave, 0)
    lax.fori_loop(0, n - 1, arrive, 0)


def local(n, regions, prior, values, precision, line, lookup, count, dist, share):
    dma = pltpu.SemaphoreType.DMA
    hbm = pl.BlockSpec(memory_space=pltpu.HBM)
    members = prior.shape[0]
    return pl.pallas_call(
        functools.partial(kernel, n, regions),
        out_shape=pltpu.VMEM(prior.shape, BF16),
        in_specs=[hbm] * 7 + [pl.BlockSpec(memory_space=pltpu.SMEM)],
        out_specs=pl.BlockSpec(memory_space=pl.ANY),
        scratch_shapes=[
            pltpu.VMEM((32, 128), jnp.int32),
            pltpu.VMEM((32, 128), BF16),
            pltpu.VMEM((32, 128), BF16),
            pltpu.VMEM((64, 128), F32),
            pltpu.VMEM(lookup.shape, jnp.int32),
            pltpu.VMEM(dist.shape, jnp.int32),
            pltpu.VMEM(share.shape, jnp.int32),
            pltpu.VMEM(prior.shape, BF16),
            pltpu.VMEM((2, 512, 1024), BF16),
            pltpu.VMEM((n, members, 256), BF16),
            pltpu.VMEM((3, 512, 256), BF16),
            pltpu.VMEM((512, 768), BF16),
            pltpu.VMEM((512, 768), BF16),
            pltpu.VMEM((32, 256), F32),
            pltpu.VMEM((2, 8, 256), F32),
            pltpu.VMEM((2, 512, 512), BF16),
            pltpu.VMEM((2, 512, 512), BF16),
            pltpu.VMEM((2, 8, 512), F32),
            pltpu.VMEM((2, 8, 512), F32),
            pltpu.VMEM((512, 512), F32),
            pltpu.VMEM((2, 512, 512), BF16),
            pltpu.VMEM((2, 512, 512), BF16),
            pltpu.VMEM((512, 512), BF16),
            pltpu.VMEM((512, 512), BF16),
            pltpu.VMEM((8, 512), F32),
            pltpu.VMEM((8, 512), F32),
            pltpu.VMEM((2, n, members, 1024), BF16),
            dma, dma((6,)), dma((2,)),
            dma((2, n)), dma((2, n)),
            dma((n,)), dma((n,)),
            dma((2,)), dma((2,)),
            dma((2,)), dma((2,)),
            dma((2, 4)), dma((2, 4)),
            dma((2,)), dma((2,)),
            dma((n,)), dma((n,)),
            dma, dma,
            dma((2, n)), dma((2, n)),
        ],
        compiler_params=pltpu.CompilerParams(
            collective_id=0, has_side_effects=True, vmem_limit_bytes=60 * 1024 * 1024
        ),
    )(prior, *(a.reshape(-1, 128) for a in (line, values, precision)), lookup, dist, share, count)


def solution(mesh):
    in_specs = (
        P("member", "region"),
        P("region"),
        P("region"),
        P("region"),
        P("region", None, None),
        P("region", "member"),
        P("region", "member", None),
        P("region", "member", None),
    )
    body = functools.partial(local, mesh.shape["member"], mesh.shape["region"])
    return jax.shard_map(body, mesh=mesh, in_specs=in_specs, out_specs=P("member", "region"), check_vma=False)
```

```python
import functools

import jax
import jax.numpy as jnp
from jax import lax
from jax.experimental import pallas as pl
from jax.experimental.pallas import tpu as pltpu
from jax.sharding import PartitionSpec as P

ITERS = 6
MESH = pl.DeviceIdType.MESH
F32 = jnp.float32
BF16 = jnp.bfloat16
NN = (((1,), (0,)), ((), ()))
NT = (((1,), (1,)), ((), ()))


def dot(a, b, dims=NN):
    return lax.dot_general(a, b, dims, preferred_element_type=F32)


def iota(shape, dim):
    return lax.broadcasted_iota(jnp.int32, shape, dim)


def split_rows(x):
    hi = x.astype(BF16).astype(F32)
    mid = (x - hi).astype(BF16).astype(F32)
    low = x - hi - mid
    row = iota((16, x.shape[1]), 0)
    rows = jnp.where(row == 0, hi, jnp.where(row == 1, mid, jnp.where(row == 2, low, 0.0)))
    return rows.astype(BF16)


def row_dot(x, b, dims):
    return jnp.sum(dot(split_rows(x), b, dims), axis=0, keepdims=True)


def kernel(
    n, regions,
    prior, line_in, values_in, precision_in, lookup_in, dist_in, share_in, count,
    out,
    line, values, precisions, data, lookup, dist, share, pv, state, psend, blocks, pert, wp, want, asked, gs, gr, vs, vr, amat, y, z, t, ye, fs, fe, res,
    load_sem, small_sem, own_sem, in_s, in_r, pr_s, pr_r, halo_s, halo_r, want_s, want_r, g_s, g_r, v_s, v_r, y_s, y_r, f_s, f_r, out_s, out_r,
):
    p = lax.axis_index("member")
    s = lax.axis_index("region")
    members = 512 // n
    west, east = lax.rem(s + regions - 1, regions), lax.rem(s + 1, regions)

    def remote(src, dst, ss, rs, **where):
        return pltpu.make_async_remote_copy(
            src_ref=src, dst_ref=dst, send_sem=ss, recv_sem=rs, device_id=where, device_id_type=MESH
        )

    def peer(d):
        return lax.rem(p + d, n)

    def nth(i):
        k = n // 2 - lax.div(i + 1, 2)
        return jnp.where(lax.rem(i, 2) == 1, k, n - k)

    def my_rows(ref, k):
        return ref.at[pl.ds(pl.multiple_of(k * members, members), members)]

    def half_band(ref, k, h):
        return ref.at[:, pl.ds(pl.multiple_of(k * 2048 + 1024 * h, 1024), 1024)]

    barrier = pltpu.get_barrier_semaphore()

    def greet(d, carry):
        pl.semaphore_signal(barrier, inc=1, device_id={"member": peer(d)}, device_id_type=MESH)
        return carry

    lax.fori_loop(1, n, greet, 0)
    for other in (west, east):
        pl.semaphore_signal(barrier, inc=1, device_id={"region": other}, device_id_type=MESH)

    load = pltpu.make_async_copy(prior, pv, load_sem)
    load.start()
    smalls = [
        pltpu.make_async_copy(src, dst, small_sem.at[k])
        for k, (src, dst) in enumerate(
            (
                (line_in, line),
                (lookup_in, lookup),
                (dist_in, dist),
                (values_in, values),
                (precision_in, precisions),
                (share_in, share),
            )
        )
    ]
    for c in smalls:
        c.start()
    def pair(ref, k):
        return jnp.concatenate([ref[pl.ds(2 * k, 1), :], ref[pl.ds(2 * k + 1, 1), :]], axis=1)

    def project(q):
        rows = [pv[:, pl.ds(pl.multiple_of(q * 2048 + 256 * h, 256), 256)] for h in range(8)]
        at = pair(line, q)
        pick = jnp.where(iota((256, 256), 0) == (at & 255), 1.0, 0.0).astype(BF16)
        found = dot(jnp.concatenate(rows, axis=0), pick)
        high = lax.shift_right_logical(at, 8) & 7
        total = jnp.zeros((members, 256), F32)
        for h in range(8):
            total = total + jnp.where(high == h, found[members * h : members * (h + 1)], 0.0)
        return total.astype(BF16)

    smalls[0].wait()
    load.wait()

    def project_one(q, carry):
        psend[q] = project(q)
        return carry

    lax.fori_loop(0, n, project_one, 0)
    pl.semaphore_wait(barrier, n + 1)

    def state_copy(d, h):
        q = peer(d)
        return remote(half_band(pv, q, h), my_rows(state.at[h], p), in_s.at[h, d], in_r.at[h, d], member=q)

    def send_state(h, pairs):
        for k in pairs:
            state_copy(k, h).start()
            if 2 * k != n:
                state_copy(n - k, h).start()

    want_west = remote(want.at[pl.ds(0, 8)], asked.at[1], want_s.at[0], want_r.at[1], region=west)
    want_east = remote(want.at[pl.ds(16, 8)], asked.at[0], want_s.at[1], want_r.at[0], region=east)

    def proj_copy(d):
        q = peer(d)
        return remote(psend.at[q], my_rows(blocks.at[1], p), pr_s.at[d], pr_r.at[d], member=q)

    def proj_send(d, carry):
        proj_copy(d).start()
        return carry

    lax.fori_loop(1, n, proj_send, 0)
    send_state(0, range(1, 4))
    blocks[1, pl.ds(pl.multiple_of(p * members, members), members), :] = psend[p]
    owns = [
        pltpu.make_async_copy(half_band(pv, p, h), my_rows(state.at[h], p), own_sem.at[h]) for h in range(2)
    ]
    for c in owns:
        c.start()

    for c in smalls[1:]:
        c.wait()
    data[0:32, :] = values[...].astype(F32)
    data[32:64, :] = precisions[...].astype(F32)

    slots = lookup.shape[-1]
    named = lookup[0, pl.ds(p, 1), :]
    side = lax.shift_right_logical(named, 12)
    offset = (lax.shift_right_logical(named, 8) & 15) - p + 1
    live = iota((1, slots), 1) < count[0, 0]
    code = jnp.where(live, (dist[0] + 1).astype(F32), 0.0)
    group = jnp.where(iota((32, slots), 0) == side * 8 + offset, code, 0.0).astype(BF16)
    place = jnp.where(iota((256, slots), 0) == (named & 255), 1.0, 0.0).astype(BF16)
    want[...] = dot(group, place, NT)

    want_west.start()
    want_east.start()

    def proj_wait(d, carry):
        proj_copy(d).wait_recv()
        return carry

    lax.fori_loop(1, n, proj_wait, 0)
    up = remote(blocks.at[1], blocks.at[0], halo_s.at[0], halo_r.at[0], member=peer(1))
    down = remote(blocks.at[1], blocks.at[2], halo_s.at[1], halo_r.at[1], member=peer(n - 1))
    up.start()
    down.start()
    send_state(0, range(n // 2, 3, -1))
    send_state(1, range(1, n // 2 + 1))

    departs, precision = [None] * 3, [None] * 3

    def centre(j):
        values = blocks[j].astype(F32)
        ybar = jnp.mean(values, axis=0, keepdims=True)
        pert[:, 256 * j : 256 * (j + 1)] = (values - ybar).astype(BF16)
        k = lax.rem(p + n - 1 + j, n)
        departs[j] = pair(data, k) - ybar
        precision[j] = pair(data, n + k)

    centre(1)
    up.wait_recv()
    centre(0)
    down.wait_recv()
    centre(2)
    want_west.wait_recv()
    want_east.wait_recv()

    def weigh(asks):
        moments = []
        for j in range(3):
            code = asks[j : j + 1, :]
            w = jnp.where(code > 0.0, precision[j] * 2.0 / (1.0 + code), 0.0)
            cols = slice(256 * j, 256 * (j + 1))
            wp[:, cols] = (pert[:, cols].astype(F32) * w).astype(BF16)
            moments.append(w * departs[j])
        return row_dot(jnp.concatenate(moments, axis=1), pert[...], NT)

    def gram(i):
        return dot(wp[128 * i : 128 * (i + 1), :], pert[128 * i :, :], NT)

    def gram_copy(side, i, where):
        part = (pl.ds(128 * i, 128), pl.ds(128 * i, 512 - 128 * i))
        return remote(gs.at[side].at[part], gr.at[1 - side].at[part], g_s.at[side, i], g_r.at[1 - side, i], region=where)

    def moment_copy(side, where):
        return remote(vs.at[side], vr.at[1 - side], v_s.at[side], v_r.at[1 - side], region=where)

    for side_, where in ((0, west), (1, east)):
        moment = weigh(asked[side_])
        vs[side_] = jnp.broadcast_to(moment, (8, 512))
        moment_copy(side_, where).start()
        for i in range(4):
            gs[side_, 128 * i : 128 * (i + 1), 128 * i :] = gram(i).astype(BF16)
            gram_copy(side_, i, where).start()
    gvec = weigh(want[8:16, :])
    for i in range(4):
        amat[128 * i : 128 * (i + 1), 128 * i :] = gram(i)

    def eye(rows, cols, at):
        return iota((rows, cols), 0) + at == iota((rows, cols), 1)

    squares = jnp.zeros((1, 1), F32)
    for i in range(4):
        for side_, where in ((0, west), (1, east)):
            gram_copy(side_, i, where).wait_recv()
        rows, width = slice(128 * i, 128 * (i + 1)), 512 - 128 * i
        a = amat[rows, 128 * i :] + (gr[0, rows, 128 * i :].astype(F32) + gr[1, rows, 128 * i :].astype(F32))
        a = a + jnp.where(eye(128, width, 0), 511.0, 0.0)
        amat[rows, 128 * i :] = a
        twice = a * a * jnp.where(iota((1, width), 1) < 128, 1.0, 2.0)
        squares = squares + jnp.sum(jnp.sum(twice, axis=0, keepdims=True), axis=1, keepdims=True)
    norm = jnp.sqrt(squares)
    inverse = 1.0 / norm
    for i in range(4):
        rows = slice(128 * i, 128 * (i + 1))
        scaled = amat[rows, 128 * i :] * inverse
        z[0, rows, 128 * i :] = scaled.astype(BF16)
        for j in range(i + 1, 4):
            z[0, 128 * j : 128 * (j + 1), rows] = scaled[:, 128 * (j - i) : 128 * (j - i + 1)].T.astype(BF16)

    half = 256
    halves = [slice(0, half), slice(half, 512)]
    for k, rows in enumerate(halves):
        first = jnp.where(eye(half, 512, half * k), 1.5, 0.0) - 0.5 * z[0, rows, :].astype(F32)
        y[1, rows, :] = first.astype(BF16)
    for rows in halves:
        z[1, rows, :] = dot(y[1, rows, :], z[0]).astype(BF16)

    def make_t(now):
        for k, rows in enumerate(halves):
            product = dot(z[now, rows, :], y[now])
            t[rows, :] = (jnp.where(eye(half, 512, half * k), 1.5, 0.0) - 0.5 * product).astype(BF16)

    def step(it, carry):
        now = lax.rem(it, 2)
        make_t(now)
        for rows in halves:
            y[1 - now, rows, :] = dot(y[now, rows, :], t[...]).astype(BF16)
            z[1 - now, rows, :] = dot(t[rows, :], z[now]).astype(BF16)
        return carry

    lax.fori_loop(1, ITERS - 1, step, 0)
    last = (ITERS - 1) % 2
    make_t(last)
    yf = y.at[1 - last]
    for rows in halves:
        yf[rows, :] = dot(y[last, rows, :], t[...]).astype(BF16)

    def east_copy(d):
        q = peer(d)
        return remote(my_rows(yf, q), my_rows(ye, q), y_s.at[d], y_r.at[d], region=west)

    def east_send(i, carry):
        east_copy(nth(i)).start()
        return carry

    lax.fori_loop(0, n - 1, east_send, 0)
    east_copy(0).start()
    for side_, where in ((0, west), (1, east)):
        moment_copy(side_, where).wait_recv()
    gvec = gvec + (vr[0, 0:1, :] + vr[1, 0:1, :])
    root = jnp.sqrt(norm)
    wbar = row_dot(row_dot(gvec, yf[...], NT) / root, yf[...], NT) / root
    scale = jnp.sqrt(F32(511.0)) / root
    fs[...] = jnp.where(iota((8, 512), 0) == 0, wbar, jnp.broadcast_to(scale, (8, 512)))
    factors = remote(fs, fe, f_s, f_r, region=west)
    factors.start()

    factors.wait_recv()
    tile = 512
    wide = jnp.concatenate(
        [split_rows(wbar), split_rows(fe[0:1, :]), jnp.ones((16, 512), BF16)], axis=0
    )
    totals = [jnp.sum(w, axis=1, keepdims=True) for w in (wbar, fe[0:1, :])]

    def out_copy(d, h):
        q = peer(d)
        return remote(res.at[h, q], half_band(out, p, h), out_s.at[h, d], out_r.at[h, d], member=q)

    mine = []
    for h in range(2):
        owns[h].wait()

        def state_wait(d, carry):
            state_copy(d, h).wait_recv()
            return carry

        lax.fori_loop(1, n, state_wait, 0)
        rules = []
        for c in range(2):
            cols = slice(tile * c, tile * (c + 1))
            part = share[0, :, 1024 * h + tile * c : 1024 * h + tile * (c + 1)].astype(F32) * 0.125
            rows = dot(wide, state[h, :, cols])
            xbar = rows[32:33] * (1.0 / 512.0)
            shifts = [
                jnp.sum(rows[16 * k : 16 * (k + 1)], axis=0, keepdims=True) - totals[k] * xbar
                for k in range(2)
            ]
            base = xbar + (1.0 - part) * shifts[0] + part * shifts[1]
            rules.append((cols, xbar, base, (1.0 - part) * scale, part * fe[1:2, 0:tile]))

        def update(q):
            at = pl.ds(pl.multiple_of(q * members, members), members)
            lhs = jnp.concatenate([yf[at, :], ye[at, :]], axis=0)
            weight = jnp.sum(lhs.astype(F32), axis=1, keepdims=True)
            for cols, xbar, base, here, there in rules:
                both = dot(lhs, state[h, :, cols]) - weight * xbar
                res[h, q, :, cols] = (base + here * both[:members] + there * both[members:]).astype(BF16)

        def update_one(i, carry):
            d = nth(i)
            if h == 0:
                east_copy(d).wait_recv()
            update(peer(d))
            out_copy(d, h).start()
            return carry

        lax.fori_loop(0, n - 1, update_one, 0)
        if h == 0:
            east_copy(0).wait_recv()
        update(p)
        mine.append(pltpu.make_async_copy(res.at[h, p], half_band(out, p, h), own_sem.at[h]))
        mine[h].start()

    def settle(d, carry):
        proj_copy(d).wait_send()
        east_copy(d).wait_send()
        for h in range(2):
            state_copy(d, h).wait_send()
        return carry

    lax.fori_loop(1, n, settle, 0)
    east_copy(0).wait_send()
    for c in (want_west, want_east, up, down, factors):
        c.wait_send()
    for side_, where in ((0, west), (1, east)):
        moment_copy(side_, where).wait_send()
        for i in range(4):
            gram_copy(side_, i, where).wait_send()
    for c in mine:
        c.wait()

    def leave(i, carry):
        for h in range(2):
            out_copy(nth(i), h).wait_send()
        out_copy(nth(i), 0).wait_recv()
        return carry

    def arrive(i, carry):
        out_copy(nth(i), 1).wait_recv()
        return carry

    lax.fori_loop(0, n - 1, leave, 0)
    lax.fori_loop(0, n - 1, arrive, 0)


def local(n, regions, prior, values, precision, line, lookup, count, dist, share):
    dma = pltpu.SemaphoreType.DMA
    hbm = pl.BlockSpec(memory_space=pltpu.HBM)
    members = prior.shape[0]
    return pl.pallas_call(
        functools.partial(kernel, n, regions),
        out_shape=pltpu.VMEM(prior.shape, BF16),
        in_specs=[hbm] * 7 + [pl.BlockSpec(memory_space=pltpu.SMEM)],
        out_specs=pl.BlockSpec(memory_space=pl.ANY),
        scratch_shapes=[
            pltpu.VMEM((32, 128), jnp.int32),
            pltpu.VMEM((32, 128), BF16),
            pltpu.VMEM((32, 128), BF16),
            pltpu.VMEM((64, 128), F32),
            pltpu.VMEM(lookup.shape, jnp.int32),
            pltpu.VMEM(dist.shape, jnp.int32),
            pltpu.VMEM(share.shape, jnp.int32),
            pltpu.VMEM(prior.shape, BF16),
            pltpu.VMEM((2, 512, 1024), BF16),
            pltpu.VMEM((n, members, 256), BF16),
            pltpu.VMEM((3, 512, 256), BF16),
            pltpu.VMEM((512, 768), BF16),
            pltpu.VMEM((512, 768), BF16),
            pltpu.VMEM((32, 256), F32),
            pltpu.VMEM((2, 8, 256), F32),
            pltpu.VMEM((2, 512, 512), BF16),
            pltpu.VMEM((2, 512, 512), BF16),
            pltpu.VMEM((2, 8, 512), F32),
            pltpu.VMEM((2, 8, 512), F32),
            pltpu.VMEM((512, 512), F32),
            pltpu.VMEM((2, 512, 512), BF16),
            pltpu.VMEM((2, 512, 512), BF16),
            pltpu.VMEM((512, 512), BF16),
            pltpu.VMEM((512, 512), BF16),
            pltpu.VMEM((8, 512), F32),
            pltpu.VMEM((8, 512), F32),
            pltpu.VMEM((2, n, members, 1024), BF16),
            dma, dma((6,)), dma((2,)),
            dma((2, n)), dma((2, n)),
            dma((n,)), dma((n,)),
            dma((2,)), dma((2,)),
            dma((2,)), dma((2,)),
            dma((2, 4)), dma((2, 4)),
            dma((2,)), dma((2,)),
            dma((n,)), dma((n,)),
            dma, dma,
            dma((2, n)), dma((2, n)),
        ],
        compiler_params=pltpu.CompilerParams(
            collective_id=0, has_side_effects=True, vmem_limit_bytes=60 * 1024 * 1024
        ),
    )(prior, *(a.reshape(-1, 128) for a in (line, values, precision)), lookup, dist, share, count)


def solution(mesh):
    in_specs = (
        P("member", "region"),
        P("region"),
        P("region"),
        P("region"),
        P("region", None, None),
        P("region", "member"),
        P("region", "member", None),
        P("region", "member", None),
    )
    body = functools.partial(local, mesh.shape["member"], mesh.shape["region"])
    return jax.shard_map(body, mesh=mesh, in_specs=in_specs, out_specs=P("member", "region"), check_vma=False)
```
